32 devices in a mesh: grp: 2 (over y), dp: 4 (over z), tp: 4 (over x, core).
Axes of the slice: x: 2, y: 2, z: 4, core: 2. Of those that a mesh axis runs over, the one named last changes fastest.
Arguments:
- dino_stream: bfloat16 [4, 256, 1536], P(None, 'dp'), may hold values from -6 to 6
- siglip_stream: bfloat16 [4, 256, 1152], P(None, 'dp'), may hold values from -6 to 6
- student_stream: bfloat16 [4, 256, 1280], P('dp'), may hold values from -6 to 6
- dino_mlp: bfloat16 [3, 1536, 4096], P(None, 'dp', 'tp'), may hold values from -0.15625 to 0.15625
- siglip_mlp: bfloat16 [2, 1152, 4304], P(None, 'dp', 'tp'), may hold values from -0.1875 to 0.1875
- student_mlp: bfloat16 [2, 1280, 5120], P(None, 'dp', 'tp'), may hold values from -0.15625 to 0.15625
- dino_head: bfloat16 [1280, 1536], P('dp', 'tp'), may hold values from -0.15625 to 0.15625
- siglip_head: bfloat16 [1280, 1152], P('dp', 'tp'), may hold values from -0.15625 to 0.15625
- assign: int32 [4], replicated, may hold values from 0 to 3, each once
Outputs:
- grad_student_mlp: float32 [2, 1280, 5120], P(None, ('grp', 'dp'), 'tp')
- grad_dino_head: float32 [1280, 1536], P(('grp', 'dp'), 'tp')
- grad_siglip_head: float32 [1280, 1152], P(('grp', 'dp'), 'tp')
The draws below stay inside these ranges and needn't reach their ends.
Inputs may be any that keep to these rules, and one draw needn't show every extreme that they name: assign names each image once.
All inputs are finite; a program needn't handle non-finite values.
Results may differ from the reference program's by a relative error of at most 0.013.
Values may be sent and summed in bfloat16 or wider, within the bound.
A program may use at most 192 MiB of HBM per device.

```python
import math
import jax
import jax.numpy as jnp
from jax import lax

D_DINO = 1536
FF_DINO = 4096
D_SIG = 1152
FF_SIG = 4304
D_STU = 1280
FF_STU = 5120
IMG_DEV = 1
PATCHES = 256
IMAGES = 4
N_DP = 4


def spiked(drawn, own_key, source, target, blocks, factor):
    owner, partner = [(jnp.arange(drawn.shape[axis_at]) // (drawn.shape[axis_at] // blocks)).reshape([-1 if axis == axis_at else 1 for axis in range(drawn.ndim)]) for axis_at in (source, target)]
    chosen = jax.random.permutation(own_key, blocks)[partner]
    strong = (owner == chosen) | (owner == (partner + blocks // 2) % blocks)
    return jnp.where(strong, factor * drawn, drawn)


def steps_of(key, shape, split, smallest, largest):
    loudness = 1.0
    for position, blocks in split:
        steps = jax.random.uniform(jax.random.fold_in(jax.random.fold_in(key, 6), position), (blocks,), jnp.float32, smallest / len(split), largest / len(split))
        loudness = loudness * jnp.repeat(jnp.exp(steps), shape[position] // blocks).reshape((-1,) + (1,) * (len(shape) - 1 - position))
    return loudness


def bell_draw(key, shape, scale, most, split=(), kind=jnp.bfloat16):
    values = jax.random.normal(key, shape, jnp.float32) * scale
    if len(split) > 0:
        values = steps_of(key, shape, split, -0.22, 0.18) * values
    return jnp.clip(values, min=-most, max=most).astype(kind)


def heavy_noise(stream_key, shape, deviation, bound, split, heavy, kind=jnp.bfloat16):
    values = deviation * jax.random.normal(stream_key, shape, jnp.float32)
    if split:
        values = values * steps_of(stream_key, shape, split, -0.22, 0.18)
    return jnp.clip(spiked(values, jax.random.fold_in(stream_key, 3), *heavy), -bound, bound).astype(kind)


def setup_inputs(seed: int = 0) -> dict:
    streams_of = jax.random.split(jax.random.key(seed), 10)
    dino_stream = bell_draw(streams_of[0], (IMAGES, PATCHES, D_DINO), 1.0, 6.0, ((1, 4),))
    siglip_stream = bell_draw(streams_of[1], (IMAGES, PATCHES, D_SIG), 1.0, 6.0, ((1, 4),))
    student_stream = heavy_noise(streams_of[2], (IMAGES, PATCHES, D_STU), 1.0, 6.0, ((0, 4),), (0, 2, 4, 2.0))
    dino_mlp = bell_draw(streams_of[3], (3, D_DINO, FF_DINO), D_DINO ** -0.5, 0.15625, ((1, 4), (2, 4)))
    siglip_mlp = bell_draw(streams_of[4], (2, D_SIG, FF_SIG), D_SIG ** -0.5, 0.1875, ((1, 4), (2, 4)))
    student_mlp = bell_draw(streams_of[5], (2, D_STU, FF_STU), D_STU ** -0.5, 0.15625, ((1, 4), (2, 4)))
    dino_head = bell_draw(streams_of[6], (D_STU, D_DINO), D_STU ** -0.5, 0.15625, ((0, 4), (1, 4)))
    siglip_head = bell_draw(streams_of[7], (D_STU, D_SIG), D_STU ** -0.5, 0.15625, ((0, 4), (1, 4)))
    assign = jax.random.permutation(streams_of[8], IMAGES).astype(jnp.int32)
    return dict(dino_stream=dino_stream, siglip_stream=siglip_stream, student_stream=student_stream, dino_mlp=dino_mlp, siglip_mlp=siglip_mlp, student_mlp=student_mlp, dino_head=dino_head, siglip_head=siglip_head, assign=assign)


def norm_rows(values):
    center = values - lax.optimization_barrier(jnp.mean(values, axis=-1, keepdims=True))
    spread = lax.optimization_barrier(jnp.mean(center * center, axis=-1, keepdims=True))
    return center * lax.rsqrt(spread + 1e-06)

def norm_back(values, upstream):
    center = values - lax.optimization_barrier(jnp.mean(values, axis=-1, keepdims=True))
    factor = lax.rsqrt(lax.optimization_barrier(jnp.mean(center * center, axis=-1, keepdims=True)) + 1e-06)
    normed = center * factor
    first = lax.optimization_barrier(jnp.mean(upstream, axis=-1, keepdims=True))
    second = lax.optimization_barrier(jnp.mean(upstream * normed, axis=-1, keepdims=True))
    return factor * (upstream - first - normed * second)

def gelu_slope(values):
    cdf = 0.5 * (1.0 + lax.erf(values * (1.0 / math.sqrt(2.0))))
    pdf = jnp.exp(-0.5 * values * values) * (1.0 / math.sqrt(2.0 * math.pi))
    return cdf + values * pdf

def reference(dino_stream, siglip_stream, student_stream, dino_mlp, siglip_mlp, student_mlp, dino_head, siglip_head, assign):

    def dino_image(image):
        normed = norm_rows(image.astype(jnp.float32)).astype(jnp.bfloat16)
        gate = jnp.dot(normed, dino_mlp[0], preferred_element_type=jnp.float32)
        upper = jnp.dot(normed, dino_mlp[1], preferred_element_type=jnp.float32)
        hidden = (jax.nn.silu(gate) * upper).astype(jnp.bfloat16)
        out = jnp.dot(hidden, dino_mlp[2].T, preferred_element_type=jnp.float32)
        return (image.astype(jnp.float32) + out).astype(jnp.bfloat16)

    def siglip_image(image):
        normed = norm_rows(image.astype(jnp.float32)).astype(jnp.bfloat16)
        first = jnp.dot(normed, siglip_mlp[0], preferred_element_type=jnp.float32)
        hidden = jax.nn.gelu(first, approximate=True).astype(jnp.bfloat16)
        out = jnp.dot(hidden, siglip_mlp[1].T, preferred_element_type=jnp.float32)
        return (image.astype(jnp.float32) + out).astype(jnp.bfloat16)
    dino_feat = lax.map(dino_image, dino_stream)
    siglip_feat = lax.map(siglip_image, siglip_stream)
    dino_target = jnp.take(dino_feat, assign, axis=0)
    siglip_target = jnp.take(siglip_feat, assign, axis=0)
    scale = 1.0 / math.sqrt(IMAGES * PATCHES)
    rows = IMG_DEV * PATCHES
    shards = (student_stream.reshape(N_DP, rows, D_STU), dino_target.reshape(N_DP, rows, D_DINO), siglip_target.reshape(N_DP, rows, D_SIG))

    def one_shard(carry, pieces):
        stream, target_d, target_s = pieces
        flat = stream.astype(jnp.float32)
        normed = norm_rows(flat).astype(jnp.bfloat16)
        act = jnp.dot(normed, student_mlp[0], preferred_element_type=jnp.float32)
        hidden = jax.nn.gelu(act, approximate=False).astype(jnp.bfloat16)
        mixed = flat + jnp.dot(hidden, student_mlp[1].T, preferred_element_type=jnp.float32)
        feat = norm_rows(mixed).astype(jnp.bfloat16)
        pred_d = jnp.dot(feat, dino_head, preferred_element_type=jnp.float32)
        pred_s = jnp.dot(feat, siglip_head, preferred_element_type=jnp.float32)
        diff_d = ((pred_d - target_d.astype(jnp.float32)) * scale).astype(jnp.bfloat16)
        diff_s = ((pred_s - target_s.astype(jnp.float32)) * scale).astype(jnp.bfloat16)
        grad_d = jnp.dot(feat.T, diff_d, preferred_element_type=jnp.float32)
        grad_s = jnp.dot(feat.T, diff_s, preferred_element_type=jnp.float32)
        dfeat = jnp.dot(diff_d, dino_head.T, preferred_element_type=jnp.float32) + jnp.dot(diff_s, siglip_head.T, preferred_element_type=jnp.float32)
        dmixed = norm_back(mixed, dfeat).astype(jnp.bfloat16)
        grad_down = jnp.dot(dmixed.T, hidden, preferred_element_type=jnp.float32)
        dhidden = jnp.dot(dmixed, student_mlp[1], preferred_element_type=jnp.float32)
        dact = (dhidden * gelu_slope(act)).astype(jnp.bfloat16)
        grad_up = jnp.dot(normed.T, dact, preferred_element_type=jnp.float32)
        grad_mlp = jnp.stack([grad_up, grad_down])
        total_mlp, total_d, total_s = carry
        total_mlp = total_mlp + grad_mlp.astype(jnp.bfloat16).astype(jnp.float32)
        total_d = total_d + grad_d.astype(jnp.bfloat16).astype(jnp.float32)
        total_s = total_s + grad_s.astype(jnp.bfloat16).astype(jnp.float32)
        return ((total_mlp, total_d, total_s), None)
    start = (jnp.zeros((2, D_STU, FF_STU), jnp.float32), jnp.zeros((D_STU, D_DINO), jnp.float32), jnp.zeros((D_STU, D_SIG), jnp.float32))
    totals, unused = lax.scan(one_shard, start, shards)
    return (totals[0], totals[1], totals[2])
```

```python
import math

import jax
import jax.numpy as jnp
from jax import lax
from jax.sharding import PartitionSpec as P


def norm_rows(values):
    center = values - jnp.mean(values, axis=-1, keepdims=True)
    spread = jnp.mean(center * center, axis=-1, keepdims=True)
    return center * lax.rsqrt(spread + 1e-06)


def norm_back(values, upstream):
    center = values - jnp.mean(values, axis=-1, keepdims=True)
    factor = lax.rsqrt(jnp.mean(center * center, axis=-1, keepdims=True) + 1e-06)
    normed = center * factor
    first = jnp.mean(upstream, axis=-1, keepdims=True)
    second = jnp.mean(upstream * normed, axis=-1, keepdims=True)
    return factor * (upstream - first - normed * second)


def gelu_slope(values):
    cdf = 0.5 * (1.0 + lax.erf(values * (1.0 / math.sqrt(2.0))))
    pdf = jnp.exp(-0.5 * values * values) * (1.0 / math.sqrt(2.0 * math.pi))
    return cdf + values * pdf


def times_transposed(left, right):
    return lax.dot_general(
        left, right, (((1,), (1,)), ((), ())), preferred_element_type=jnp.float32
    )


def over_rows(left, right):
    return lax.dot_general(
        left, right, (((0,), (0,)), ((), ())), preferred_element_type=jnp.float32
    )


def gathered_rows(block, axis):
    count = lax.axis_size("dp")
    if count > 8:
        return lax.all_gather(block, "dp", axis=axis, tiled=True)
    up, down = [block], [block]
    for step in range(1, count):
        up.append(lax.ppermute(up[-1], "dp", [(i, i + 1) for i in range(step - 1, count - 1)]))
        down.append(
            lax.ppermute(down[-1], "dp", [(i, i - 1) for i in range(1, count - step + 1)])
        )
    line = jnp.concatenate(up[:0:-1] + down, axis=axis)
    length = block.shape[axis]
    start = (count - 1 - lax.axis_index("dp")) * length
    return lax.dynamic_slice_in_dim(line, start, count * length, axis)


def own_units(weights, group, low):
    count = weights.shape[-1]
    return jnp.where(group == 0, weights[..., : count - low], weights[..., low:])


def across(array):
    return lax.ppermute(array, "grp", [(0, 1), (1, 0)])


def body(
    dino_stream,
    siglip_stream,
    student_stream,
    dino_mlp,
    siglip_mlp,
    student_mlp,
    dino_head,
    siglip_head,
    assign,
):
    bf16, f32 = jnp.bfloat16, jnp.float32
    group = lax.axis_index("grp")
    column = lax.axis_index("tp")
    count_dp = lax.axis_size("dp")
    count_tp = lax.axis_size("tp")
    img_dev, patches, width = student_stream.shape
    rows = img_dev * patches
    images, slab, width_d = dino_stream.shape
    width_s = siglip_stream.shape[2]
    cols_d = dino_head.shape[1]
    cols_s = siglip_head.shape[1]
    units = student_mlp.shape[2] // 2
    half = width // 2
    block = half // count_dp
    scale = 1.0 / math.sqrt(images * patches)

    low_d = dino_mlp.shape[2] // 2 // 128 * 128
    low_s = siglip_mlp.shape[2] // 2 // 128 * 128
    dino_full = gathered_rows(own_units(dino_mlp, group, low_d), 1)
    siglip_full = gathered_rows(own_units(siglip_mlp, group, low_s), 1)
    w_mlp = gathered_rows(own_units(student_mlp, group, units), 1)
    w_dino = gathered_rows(dino_head, 0)
    w_sig = gathered_rows(siglip_head, 0)

    def once(hidden, low):
        place = lax.broadcasted_iota(jnp.int32, hidden.shape, 1)
        return jnp.where((group == 1) | (place < low), hidden, jnp.zeros_like(hidden))

    normed_d = norm_rows(dino_stream.reshape(images * slab, width_d).astype(f32)).astype(bf16)
    gate = jnp.dot(normed_d, dino_full[0], preferred_element_type=f32)
    upper = jnp.dot(normed_d, dino_full[1], preferred_element_type=f32)
    hidden_d = once((jax.nn.silu(gate) * upper).astype(bf16), low_d)
    part_d = times_transposed(hidden_d, dino_full[2]).astype(bf16)
    normed_s = norm_rows(siglip_stream.reshape(images * slab, width_s).astype(f32)).astype(bf16)
    first = jnp.dot(normed_s, siglip_full[0], preferred_element_type=f32)
    hidden_s = once(jax.nn.gelu(first, approximate=True).astype(bf16), low_s)
    part_s = times_transposed(hidden_s, siglip_full[1]).astype(bf16)
    parts = jnp.stack(
        [
            jnp.concatenate(
                [
                    part_d[:, i * cols_d : (i + 1) * cols_d],
                    part_s[:, i * cols_s : (i + 1) * cols_s],
                ],
                axis=1,
            )
            for i in range(count_tp)
        ]
    )
    summed = lax.psum_scatter(parts, "tp", scatter_dimension=0, tiled=True)[0].astype(bf16)
    summed = summed.astype(f32) + across(summed).astype(f32)
    own = jnp.concatenate(
        [
            lax.dynamic_slice_in_dim(dino_stream, column * cols_d, cols_d, 2),
            lax.dynamic_slice_in_dim(siglip_stream, column * cols_s, cols_s, 2),
        ],
        axis=2,
    )
    features = (own.astype(f32) + summed.reshape(own.shape)).astype(bf16)
    arranged = jnp.take(features, assign, axis=0)
    target = lax.all_to_all(arranged, "dp", split_axis=0, concat_axis=1, tiled=True)
    target = target.reshape(rows, cols_d + cols_s).astype(f32)

    flat = student_stream.reshape(rows, width).astype(f32)
    normed = norm_rows(flat).astype(bf16)
    act = jnp.dot(normed, w_mlp[0], preferred_element_type=f32)
    hidden = jax.nn.gelu(act, approximate=False).astype(bf16)
    partial_out = times_transposed(hidden, w_mlp[1])
    mixed = flat + lax.psum(partial_out.astype(bf16), ("grp", "tp")).astype(f32)
    feat = norm_rows(mixed).astype(bf16)
    pred_d = jnp.dot(feat, w_dino, preferred_element_type=f32)
    pred_s = jnp.dot(feat, w_sig, preferred_element_type=f32)
    diff_d = ((pred_d - target[:, :cols_d]) * scale).astype(bf16)
    diff_s = ((pred_s - target[:, cols_d:]) * scale).astype(bf16)

    dfeat = times_transposed(diff_d, w_dino) + times_transposed(diff_s, w_sig)
    dfeat = lax.psum(dfeat.astype(bf16), "tp").astype(f32)
    own_feat = lax.dynamic_slice_in_dim(feat, group * half, half, 1)
    grad_heads = over_rows(own_feat, jnp.concatenate([diff_d, diff_s], axis=1)).astype(bf16)
    sum_heads = lax.psum_scatter(grad_heads, "dp", scatter_dimension=0, tiled=True).astype(f32)
    dmixed = norm_back(mixed, dfeat).astype(bf16)
    grad_down = over_rows(dmixed, hidden).astype(bf16)
    dhidden = jnp.dot(dmixed, w_mlp[1], preferred_element_type=f32)
    dact = (dhidden * gelu_slope(act)).astype(bf16)
    grad_up = over_rows(normed, dact).astype(bf16)

    def ordered(grad):
        return grad.reshape(2, count_dp, block, units).transpose(1, 0, 2, 3).reshape(width, units)

    grad_mlp = jnp.stack([ordered(grad_up), ordered(grad_down)])
    sum_mlp = lax.psum_scatter(grad_mlp, "dp", scatter_dimension=1, tiled=True)
    sum_mlp = sum_mlp.reshape(2, 2, block, units)
    away = across(jnp.where(group == 0, sum_mlp[:, 1], sum_mlp[:, 0]).astype(bf16)).astype(f32)
    here = jnp.where(group == 0, sum_mlp[:, 0], sum_mlp[:, 1]).astype(f32)
    left = jnp.where(group == 0, here, away)
    right = jnp.where(group == 0, away, here)
    return (
        jnp.concatenate([left, right], axis=2),
        sum_heads[:, :cols_d],
        sum_heads[:, cols_d:],
    )


def solution(mesh):
    in_specs = (
        P(None, "dp", None),
        P(None, "dp", None),
        P("dp", None, None),
        P(None, "dp", "tp"),
        P(None, "dp", "tp"),
        P(None, "dp", "tp"),
        P("dp", "tp"),
        P("dp", "tp"),
        P(),
    )
    out_specs = (P(None, ("grp", "dp"), "tp"), P(("grp", "dp"), "tp"), P(("grp", "dp"), "tp"))
    return jax.shard_map(body, mesh=mesh, in_specs=in_specs, out_specs=out_specs, check_vma=False)
```

```python
import math

import jax
import jax.numpy as jnp
from jax import lax
from jax.sharding import PartitionSpec as P


def norm_rows(values):
    center = values - jnp.mean(values, axis=-1, keepdims=True)
    spread = jnp.mean(center * center, axis=-1, keepdims=True)
    return center * lax.rsqrt(spread + 1e-06)


def norm_back(values, upstream):
    center = values - jnp.mean(values, axis=-1, keepdims=True)
    factor = lax.rsqrt(jnp.mean(center * center, axis=-1, keepdims=True) + 1e-06)
    normed = center * factor
    first = jnp.mean(upstream, axis=-1, keepdims=True)
    second = jnp.mean(upstream * normed, axis=-1, keepdims=True)
    return factor * (upstream - first - normed * second)


def gelu_slope(values):
    cdf = 0.5 * (1.0 + lax.erf(values * (1.0 / math.sqrt(2.0))))
    pdf = jnp.exp(-0.5 * values * values) * (1.0 / math.sqrt(2.0 * math.pi))
    return cdf + values * pdf


def times_transposed(left, right):
    return lax.dot_general(
        left, right, (((1,), (1,)), ((), ())), preferred_element_type=jnp.float32
    )


def over_rows(left, right):
    return lax.dot_general(
        left, right, (((0,), (0,)), ((), ())), preferred_element_type=jnp.float32
    )


def gathered_rows(block, axis):
    count = lax.axis_size("dp")
    if count > 8:
        return lax.all_gather(block, "dp", axis=axis, tiled=True)
    up, down = [block], [block]
    for step in range(1, count):
        up.append(lax.ppermute(up[-1], "dp", [(i, i + 1) for i in range(step - 1, count - 1)]))
        down.append(
            lax.ppermute(down[-1], "dp", [(i, i - 1) for i in range(1, count - step + 1)])
        )
    line = jnp.concatenate(up[:0:-1] + down, axis=axis)
    length = block.shape[axis]
    start = (count - 1 - lax.axis_index("dp")) * length
    return lax.dynamic_slice_in_dim(line, start, count * length, axis)


def own_units(weights, group, low):
    count = weights.shape[-1]
    return jnp.where(group == 0, weights[..., : count - low], weights[..., low:])


def summed_piece(pieces, axis):
    count = lax.axis_size(axis)
    if count > 8:
        return lax.psum_scatter(pieces, axis, scatter_dimension=0).astype(jnp.float32)
    me = lax.axis_index(axis)
    total = lax.dynamic_index_in_dim(pieces, me, 0, keepdims=False).astype(jnp.float32)
    for step in range(1, count):
        piece = lax.dynamic_index_in_dim(pieces, (me + step) % count, 0, keepdims=False)
        pairs = [(i, (i + step) % count) for i in range(count)]
        total = total + lax.ppermute(piece, axis, pairs).astype(jnp.float32)
    return total


def joined_pieces(piece, axis):
    count = lax.axis_size(axis)
    if count > 8:
        return lax.all_gather(piece, axis, axis=0)
    got = [piece]
    for step in range(1, count):
        got.append(lax.ppermute(piece, axis, [(i, (i + step) % count) for i in range(count)]))
    got = got[::-1]
    line = jnp.stack(got + got[:-1])
    return lax.dynamic_slice_in_dim(line, count - 1 - lax.axis_index(axis), count, 0)


def across(array):
    return lax.ppermute(array, "grp", [(0, 1), (1, 0)])


def body(
    dino_stream,
    siglip_stream,
    student_stream,
    dino_mlp,
    siglip_mlp,
    student_mlp,
    dino_head,
    siglip_head,
    assign,
):
    bf16, f32 = jnp.bfloat16, jnp.float32
    group = lax.axis_index("grp")
    column = lax.axis_index("tp")
    count_dp = lax.axis_size("dp")
    count_tp = lax.axis_size("tp")
    img_dev, patches, width = student_stream.shape
    rows = img_dev * patches
    images, slab, width_d = dino_stream.shape
    width_s = siglip_stream.shape[2]
    cols_d = dino_head.shape[1]
    cols_s = siglip_head.shape[1]
    units = student_mlp.shape[2] // 2
    half = width // 2
    block = half // count_dp
    scale = 1.0 / math.sqrt(images * patches)

    low_d = dino_mlp.shape[2] // 2 // 128 * 128
    low_s = siglip_mlp.shape[2] // 2 // 128 * 128
    dino_full = gathered_rows(own_units(dino_mlp, group, low_d), 1)
    siglip_full = gathered_rows(own_units(siglip_mlp, group, low_s), 1)
    w_mlp = gathered_rows(own_units(student_mlp, group, units), 1)
    w_dino = gathered_rows(dino_head, 0)
    w_sig = gathered_rows(siglip_head, 0)

    def once(hidden, low):
        place = lax.broadcasted_iota(jnp.int32, hidden.shape, 1)
        return jnp.where((group == 1) | (place < low), hidden, jnp.zeros_like(hidden))

    normed_d = norm_rows(dino_stream.reshape(images * slab, width_d).astype(f32)).astype(bf16)
    gate = jnp.dot(normed_d, dino_full[0], preferred_element_type=f32)
    upper = jnp.dot(normed_d, dino_full[1], preferred_element_type=f32)
    hidden_d = once((jax.nn.silu(gate) * upper).astype(bf16), low_d)
    part_d = times_transposed(hidden_d, dino_full[2]).astype(bf16)
    normed_s = norm_rows(siglip_stream.reshape(images * slab, width_s).astype(f32)).astype(bf16)
    first = jnp.dot(normed_s, siglip_full[0], preferred_element_type=f32)
    hidden_s = once(jax.nn.gelu(first, approximate=True).astype(bf16), low_s)
    part_s = times_transposed(hidden_s, siglip_full[1]).astype(bf16)
    parts = jnp.stack(
        [
            jnp.concatenate(
                [
                    part_d[:, i * cols_d : (i + 1) * cols_d],
                    part_s[:, i * cols_s : (i + 1) * cols_s],
                ],
                axis=1,
            )
            for i in range(count_tp)
        ]
    )
    summed = summed_piece(parts, "tp").astype(bf16)
    summed = summed.astype(f32) + across(summed).astype(f32)
    own = jnp.concatenate(
        [
            lax.dynamic_slice_in_dim(dino_stream, column * cols_d, cols_d, 2),
            lax.dynamic_slice_in_dim(siglip_stream, column * cols_s, cols_s, 2),
        ],
        axis=2,
    )
    features = (own.astype(f32) + summed.reshape(own.shape)).astype(bf16)
    arranged = jnp.take(features, assign, axis=0)
    target = lax.all_to_all(arranged, "dp", split_axis=0, concat_axis=1, tiled=True)
    target = target.reshape(rows, cols_d + cols_s).astype(f32)

    flat = student_stream.reshape(rows, width).astype(f32)
    normed = norm_rows(flat).astype(bf16)
    act = jnp.dot(normed, w_mlp[0], preferred_element_type=f32)
    hidden = jax.nn.gelu(act, approximate=False).astype(bf16)
    partial_out = times_transposed(hidden, w_mlp[1])
    mixed = flat + lax.psum(partial_out.astype(bf16), ("grp", "tp")).astype(f32)
    feat = norm_rows(mixed).astype(bf16)
    pred_d = jnp.dot(feat, w_dino, preferred_element_type=f32)
    pred_s = jnp.dot(feat, w_sig, preferred_element_type=f32)
    diff_d = ((pred_d - target[:, :cols_d]) * scale).astype(bf16)
    diff_s = ((pred_s - target[:, cols_d:]) * scale).astype(bf16)

    dfeat = times_transposed(diff_d, w_dino) + times_transposed(diff_s, w_sig)
    dfeat = summed_piece(dfeat.astype(bf16).reshape(count_tp, rows // count_tp, width), "tp")
    own_mixed = lax.dynamic_slice_in_dim(
        mixed, column * (rows // count_tp), rows // count_tp, 0
    )
    dmixed = joined_pieces(norm_back(own_mixed, dfeat).astype(bf16), "tp").reshape(rows, width)
    own_feat = lax.dynamic_slice_in_dim(feat, group * half, half, 1)
    grad_heads = over_rows(own_feat, jnp.concatenate([diff_d, diff_s], axis=1)).astype(bf16)
    sum_heads = summed_piece(grad_heads.reshape(count_dp, block, cols_d + cols_s), "dp")
    grad_down = over_rows(dmixed, hidden).astype(bf16)
    dhidden = jnp.dot(dmixed, w_mlp[1], preferred_element_type=f32)
    dact = (dhidden * gelu_slope(act)).astype(bf16)
    grad_up = over_rows(normed, dact).astype(bf16)

    def ordered(grad):
        return grad.reshape(2, count_dp, block, units).transpose(1, 0, 2, 3).reshape(width, units)

    grad_mlp = jnp.stack([ordered(grad_up), ordered(grad_down)])
    sum_mlp = lax.psum_scatter(grad_mlp, "dp", scatter_dimension=1, tiled=True)
    sum_mlp = sum_mlp.reshape(2, 2, block, units)
    away = across(jnp.where(group == 0, sum_mlp[:, 1], sum_mlp[:, 0]).astype(bf16)).astype(f32)
    here = jnp.where(group == 0, sum_mlp[:, 0], sum_mlp[:, 1]).astype(f32)
    left = jnp.where(group == 0, here, away)
    right = jnp.where(group == 0, away, here)
    return (
        jnp.concatenate([left, right], axis=2),
        sum_heads[:, :cols_d],
        sum_heads[:, cols_d:],
    )


def solution(mesh):
    in_specs = (
        P(None, "dp", None),
        P(None, "dp", None),
        P("dp", None, None),
        P(None, "dp", "tp"),
        P(None, "dp", "tp"),
        P(None, "dp", "tp"),
        P("dp", "tp"),
        P("dp", "tp"),
        P(),
    )
    out_specs = (P(None, ("grp", "dp"), "tp"), P(("grp", "dp"), "tp"), P(("grp", "dp"), "tp"))
    return jax.shard_map(body, mesh=mesh, in_specs=in_specs, out_specs=out_specs, check_vma=False)
```

```python
import math

import jax
import jax.numpy as jnp
from jax import lax
from jax.sharding import PartitionSpec as P


def norm_rows(values):
    center = values - jnp.mean(values, axis=-1, keepdims=True)
    spread = jnp.mean(center * center, axis=-1, keepdims=True)
    return center * lax.rsqrt(spread + 1e-06)


def norm_back(values, upstream):
    center = values - jnp.mean(values, axis=-1, keepdims=True)
    factor = lax.rsqrt(jnp.mean(center * center, axis=-1, keepdims=True) + 1e-06)
    normed = center * factor
    first = jnp.mean(upstream, axis=-1, keepdims=True)
    second = jnp.mean(upstream * normed, axis=-1, keepdims=True)
    return factor * (upstream - first - normed * second)


def gelu_slope(values):
    cdf = 0.5 * (1.0 + lax.erf(values * (1.0 / math.sqrt(2.0))))
    pdf = jnp.exp(-0.5 * values * values) * (1.0 / math.sqrt(2.0 * math.pi))
    return cdf + values * pdf


def times_transposed(left, right):
    return lax.dot_general(
        left, right, (((1,), (1,)), ((), ())), preferred_element_type=jnp.float32
    )


def over_rows(left, right):
    return lax.dot_general(
        left, right, (((0,), (0,)), ((), ())), preferred_element_type=jnp.float32
    )


def gathered_rows(block, axis, held=()):
    count = lax.axis_size("dp")
    if count > 8:
        return (lax.all_gather(block, "dp", axis=axis, tiled=True), *held)
    up, down = [block], [block]
    for step in range(1, count):
        if held and step == count - 1:
            up[-1], down[-1], *held = lax.optimization_barrier((up[-1], down[-1], *held))
        up.append(lax.ppermute(up[-1], "dp", [(i, i + 1) for i in range(step - 1, count - 1)]))
        down.append(
            lax.ppermute(down[-1], "dp", [(i, i - 1) for i in range(1, count - step + 1)])
        )
    line = jnp.concatenate(up[:0:-1] + down, axis=axis)
    length = block.shape[axis]
    start = (count - 1 - lax.axis_index("dp")) * length
    return (lax.dynamic_slice_in_dim(line, start, count * length, axis), *held)


def own_units(weights, group, low):
    count = weights.shape[-1]
    return jnp.where(group == 0, weights[..., : count - low], weights[..., low:])


def summed_piece(pieces, axis):
    count = lax.axis_size(axis)
    if count > 8:
        return lax.psum_scatter(pieces, axis, scatter_dimension=0).astype(jnp.float32)
    me = lax.axis_index(axis)
    total = lax.dynamic_index_in_dim(pieces, me, 0, keepdims=False).astype(jnp.float32)
    for step in range(1, count):
        piece = lax.dynamic_index_in_dim(pieces, (me + step) % count, 0, keepdims=False)
        pairs = [(i, (i + step) % count) for i in range(count)]
        total = total + lax.ppermute(piece, axis, pairs).astype(jnp.float32)
    return total


def joined_pieces(piece, axis):
    count = lax.axis_size(axis)
    if count > 8:
        return lax.all_gather(piece, axis, axis=0)
    got = [piece]
    for step in range(1, count):
        got.append(lax.ppermute(piece, axis, [(i, (i + step) % count) for i in range(count)]))
    got = got[::-1]
    line = jnp.stack(got + got[:-1])
    return lax.dynamic_slice_in_dim(line, count - 1 - lax.axis_index(axis), count, 0)


def across(array):
    return lax.ppermute(array, "grp", [(0, 1), (1, 0)])


def body(
    dino_stream,
    siglip_stream,
    student_stream,
    dino_mlp,
    siglip_mlp,
    student_mlp,
    dino_head,
    siglip_head,
    assign,
):
    bf16, f32 = jnp.bfloat16, jnp.float32
    group = lax.axis_index("grp")
    column = lax.axis_index("tp")
    count_dp = lax.axis_size("dp")
    count_tp = lax.axis_size("tp")
    img_dev, patches, width = student_stream.shape
    rows = img_dev * patches
    images, slab, width_d = dino_stream.shape
    width_s = siglip_stream.shape[2]
    cols_d = dino_head.shape[1]
    cols_s = siglip_head.shape[1]
    units = student_mlp.shape[2] // 2
    half = width // 2
    block = half // count_dp
    scale = 1.0 / math.sqrt(images * patches)

    low_d = dino_mlp.shape[2] // 2 // 128 * 128
    low_s = siglip_mlp.shape[2] // 2 // 128 * 128
    own_dino = own_units(dino_mlp, group, low_d)
    own_siglip = own_units(siglip_mlp, group, low_s)
    own_student = own_units(student_mlp, group, units)
    w_mlp, own_dino, own_siglip = gathered_rows(own_student, 1, (own_dino, own_siglip))
    siglip_full, = gathered_rows(own_siglip, 1)
    dino_full, own_hd, own_hs = gathered_rows(own_dino, 1, (dino_head, siglip_head))
    w_dino, = gathered_rows(own_hd, 0)
    w_sig, = gathered_rows(own_hs, 0)

    def once(hidden, low):
        place = lax.broadcasted_iota(jnp.int32, hidden.shape, 1)
        return jnp.where((group == 1) | (place < low), hidden, jnp.zeros_like(hidden))

    normed_d = norm_rows(dino_stream.reshape(images * slab, width_d).astype(f32)).astype(bf16)
    gate = jnp.dot(normed_d, dino_full[0], preferred_element_type=f32)
    upper = jnp.dot(normed_d, dino_full[1], preferred_element_type=f32)
    hidden_d = once((jax.nn.silu(gate) * upper).astype(bf16), low_d)
    part_d = times_transposed(hidden_d, dino_full[2]).astype(bf16)
    normed_s = norm_rows(siglip_stream.reshape(images * slab, width_s).astype(f32)).astype(bf16)
    first = jnp.dot(normed_s, siglip_full[0], preferred_element_type=f32)
    hidden_s = once(jax.nn.gelu(first, approximate=True).astype(bf16), low_s)
    part_s = times_transposed(hidden_s, siglip_full[1]).astype(bf16)
    parts = jnp.stack(
        [
            jnp.concatenate(
                [
                    part_d[:, i * cols_d : (i + 1) * cols_d],
                    part_s[:, i * cols_s : (i + 1) * cols_s],
                ],
                axis=1,
            )
            for i in range(count_tp)
        ]
    )
    summed = summed_piece(parts, "tp").astype(bf16)
    summed = summed.astype(f32) + across(summed).astype(f32)
    own = jnp.concatenate(
        [
            lax.dynamic_slice_in_dim(dino_stream, column * cols_d, cols_d, 2),
            lax.dynamic_slice_in_dim(siglip_stream, column * cols_s, cols_s, 2),
        ],
        axis=2,
    )
    features = (own.astype(f32) + summed.reshape(own.shape)).astype(bf16)
    arranged = jnp.take(features, assign, axis=0)
    target = lax.all_to_all(arranged, "dp", split_axis=0, concat_axis=1, tiled=True)
    target = target.reshape(rows, cols_d + cols_s).astype(f32)

    flat = student_stream.reshape(rows, width).astype(f32)
    normed = norm_rows(flat).astype(bf16)
    act = jnp.dot(normed, w_mlp[0], preferred_element_type=f32)
    hidden = jax.nn.gelu(act, approximate=False).astype(bf16)
    partial_out = times_transposed(hidden, w_mlp[1])
    mixed = flat + lax.psum(partial_out.astype(bf16), ("grp", "tp")).astype(f32)
    feat = norm_rows(mixed).astype(bf16)
    pred_d = jnp.dot(feat, w_dino, preferred_element_type=f32)
    pred_s = jnp.dot(feat, w_sig, preferred_element_type=f32)
    diff_d = ((pred_d - target[:, :cols_d]) * scale).astype(bf16)
    diff_s = ((pred_s - target[:, cols_d:]) * scale).astype(bf16)

    dfeat = times_transposed(diff_d, w_dino) + times_transposed(diff_s, w_sig)
    dfeat = summed_piece(dfeat.astype(bf16).reshape(count_tp, rows // count_tp, width), "tp")
    own_mixed = lax.dynamic_slice_in_dim(
        mixed, column * (rows // count_tp), rows // count_tp, 0
    )
    dmixed = joined_pieces(norm_back(own_mixed, dfeat).astype(bf16), "tp").reshape(rows, width)
    own_feat = lax.dynamic_slice_in_dim(feat, group * half, half, 1)
    grad_heads = over_rows(own_feat, jnp.concatenate([diff_d, diff_s], axis=1)).astype(bf16)
    sum_heads = summed_piece(grad_heads.reshape(count_dp, block, cols_d + cols_s), "dp")
    grad_down = over_rows(dmixed, hidden).astype(bf16)
    dhidden = jnp.dot(dmixed, w_mlp[1], preferred_element_type=f32)
    dact = (dhidden * gelu_slope(act)).astype(bf16)
    grad_up = over_rows(normed, dact).astype(bf16)

    def ordered(grad):
        return grad.reshape(2, count_dp, block, units).transpose(1, 0, 2, 3).reshape(width, units)

    grad_mlp = jnp.stack([ordered(grad_up), ordered(grad_down)])
    grad_mlp, sum_heads = lax.optimization_barrier((grad_mlp, sum_heads))
    sum_mlp = lax.psum_scatter(grad_mlp, "dp", scatter_dimension=1, tiled=True)
    sum_mlp = sum_mlp.reshape(2, 2, block, units)
    away = across(jnp.where(group == 0, sum_mlp[:, 1], sum_mlp[:, 0]).astype(bf16)).astype(f32)
    here = jnp.where(group == 0, sum_mlp[:, 0], sum_mlp[:, 1]).astype(f32)
    left = jnp.where(group == 0, here, away)
    right = jnp.where(group == 0, away, here)
    return (
        jnp.concatenate([left, right], axis=2),
        sum_heads[:, :cols_d],
        sum_heads[:, cols_d:],
    )


def solution(mesh):
    in_specs = (
        P(None, "dp", None),
        P(None, "dp", None),
        P("dp", None, None),
        P(None, "dp", "tp"),
        P(None, "dp", "tp"),
        P(None, "dp", "tp"),
        P("dp", "tp"),
        P("dp", "tp"),
        P(),
    )
    out_specs = (P(None, ("grp", "dp"), "tp"), P(("grp", "dp"), "tp"), P(("grp", "dp"), "tp"))
    return jax.shard_map(body, mesh=mesh, in_specs=in_specs, out_specs=out_specs, check_vma=False)
```

```python
import math

import jax
import jax.numpy as jnp
from jax import lax
from jax.sharding import PartitionSpec as P


def norm_rows(values):
    center = values - jnp.mean(values, axis=-1, keepdims=True)
    spread = jnp.mean(center * center, axis=-1, keepdims=True)
    return center * lax.rsqrt(spread + 1e-06)


def norm_back(values, upstream):
    center = values - jnp.mean(values, axis=-1, keepdims=True)
    factor = lax.rsqrt(jnp.mean(center * center, axis=-1, keepdims=True) + 1e-06)
    normed = center * factor
    first = jnp.mean(upstream, axis=-1, keepdims=True)
    second = jnp.mean(upstream * normed, axis=-1, keepdims=True)
    return factor * (upstream - first - normed * second)


def gelu_slope(values):
    cdf = 0.5 * (1.0 + lax.erf(values * (1.0 / math.sqrt(2.0))))
    pdf = jnp.exp(-0.5 * values * values) * (1.0 / math.sqrt(2.0 * math.pi))
    return cdf + values * pdf


def times_transposed(left, right):
    return lax.dot_general(
        left, right, (((1,), (1,)), ((), ())), preferred_element_type=jnp.float32
    )


def over_rows(left, right):
    return lax.dot_general(
        left, right, (((0,), (0,)), ((), ())), preferred_element_type=jnp.float32
    )


def gathered_rows(block, axis, held=()):
    count = lax.axis_size("dp")
    if count > 8:
        return (lax.all_gather(block, "dp", axis=axis, tiled=True), *held)
    up, down = [block], [block]
    for step in range(1, count):
        if held and step == count - 1:
            up[-1], down[-1], *held = lax.optimization_barrier((up[-1], down[-1], *held))
        up.append(lax.ppermute(up[-1], "dp", [(i, i + 1) for i in range(step - 1, count - 1)]))
        down.append(
            lax.ppermute(down[-1], "dp", [(i, i - 1) for i in range(1, count - step + 1)])
        )
    line = jnp.concatenate(up[:0:-1] + down, axis=axis)
    length = block.shape[axis]
    start = (count - 1 - lax.axis_index("dp")) * length
    return (lax.dynamic_slice_in_dim(line, start, count * length, axis), *held)


def own_units(weights, group, low):
    count = weights.shape[-1]
    return jnp.where(group == 0, weights[..., : count - low], weights[..., low:])


def summed_piece(pieces, axis):
    count = lax.axis_size(axis)
    if count > 8:
        return lax.psum_scatter(pieces, axis, scatter_dimension=0).astype(jnp.float32)
    me = lax.axis_index(axis)
    total = lax.dynamic_index_in_dim(pieces, me, 0, keepdims=False).astype(jnp.float32)
    for step in range(1, count):
        piece = lax.dynamic_index_in_dim(pieces, (me + step) % count, 0, keepdims=False)
        pairs = [(i, (i + step) % count) for i in range(count)]
        total = total + lax.ppermute(piece, axis, pairs).astype(jnp.float32)
    return total


def joined_pieces(piece, axis):
    count = lax.axis_size(axis)
    if count > 8:
        return lax.all_gather(piece, axis, axis=0)
    got = [piece]
    for step in range(1, count):
        got.append(lax.ppermute(piece, axis, [(i, (i + step) % count) for i in range(count)]))
    got = got[::-1]
    line = jnp.stack(got + got[:-1])
    return lax.dynamic_slice_in_dim(line, count - 1 - lax.axis_index(axis), count, 0)


def across(array):
    return lax.ppermute(array, "grp", [(0, 1), (1, 0)])


def body(
    dino_stream,
    siglip_stream,
    student_stream,
    dino_mlp,
    siglip_mlp,
    student_mlp,
    dino_head,
    siglip_head,
    assign,
):
    bf16, f32 = jnp.bfloat16, jnp.float32
    group = lax.axis_index("grp")
    column = lax.axis_index("tp")
    count_dp = lax.axis_size("dp")
    count_tp = lax.axis_size("tp")
    img_dev, patches, width = student_stream.shape
    rows = img_dev * patches
    images, slab, width_d = dino_stream.shape
    width_s = siglip_stream.shape[2]
    cols_d = dino_head.shape[1]
    cols_s = siglip_head.shape[1]
    units = student_mlp.shape[2] // 2
    half = width // 2
    block = half // count_dp
    scale = 1.0 / math.sqrt(images * patches)

    low_d = dino_mlp.shape[2] // 2 // 128 * 128
    low_s = siglip_mlp.shape[2] // 2 // 128 * 128
    own_dino = own_units(dino_mlp, group, low_d)
    own_siglip = own_units(siglip_mlp, group, low_s)
    own_student = own_units(student_mlp, group, units)
    w_mlp, own_dino, own_siglip = gathered_rows(own_student, 1, (own_dino, own_siglip))
    siglip_full, = gathered_rows(own_siglip, 1)
    dino_full, own_hd, own_hs = gathered_rows(own_dino, 1, (dino_head, siglip_head))
    w_dino, = gathered_rows(own_hd, 0)
    w_sig, = gathered_rows(own_hs, 0)

    def once(hidden, low):
        place = lax.broadcasted_iota(jnp.int32, hidden.shape, 1)
        return jnp.where((group == 1) | (place < low), hidden, jnp.zeros_like(hidden))

    normed_d = norm_rows(dino_stream.reshape(images * slab, width_d).astype(f32)).astype(bf16)
    gate = jnp.dot(normed_d, dino_full[0], preferred_element_type=f32)
    upper = jnp.dot(normed_d, dino_full[1], preferred_element_type=f32)
    hidden_d = once((jax.nn.silu(gate) * upper).astype(bf16), low_d)
    part_d = times_transposed(hidden_d, dino_full[2]).astype(bf16)
    normed_s = norm_rows(siglip_stream.reshape(images * slab, width_s).astype(f32)).astype(bf16)
    first = jnp.dot(normed_s, siglip_full[0], preferred_element_type=f32)
    hidden_s = once(jax.nn.gelu(first, approximate=True).astype(bf16), low_s)
    part_s = times_transposed(hidden_s, siglip_full[1]).astype(bf16)
    parts = jnp.stack(
        [
            jnp.concatenate(
                [
                    part_d[:, i * cols_d : (i + 1) * cols_d],
                    part_s[:, i * cols_s : (i + 1) * cols_s],
                ],
                axis=1,
            )
            for i in range(count_tp)
        ]
    )
    summed = summed_piece(parts, "tp").astype(bf16)
    summed = summed.astype(f32) + across(summed).astype(f32)
    own = jnp.concatenate(
        [
            lax.dynamic_slice_in_dim(dino_stream, column * cols_d, cols_d, 2),
            lax.dynamic_slice_in_dim(siglip_stream, column * cols_s, cols_s, 2),
        ],
        axis=2,
    )
    features = (own.astype(f32) + summed.reshape(own.shape)).astype(bf16)
    arranged = jnp.take(features, assign, axis=0)
    target = lax.all_to_all(arranged, "dp", split_axis=0, concat_axis=1, tiled=True)
    target = target.reshape(rows, cols_d + cols_s).astype(f32)

    flat = student_stream.reshape(rows, width).astype(f32)
    normed = norm_rows(flat).astype(bf16)
    act = jnp.dot(normed, w_mlp[0], preferred_element_type=f32)
    hidden = jax.nn.gelu(act, approximate=False).astype(bf16)
    partial_out = times_transposed(hidden, w_mlp[1])
    share = rows // count_tp
    out = summed_piece(partial_out.astype(bf16).reshape(count_tp, share, width), "tp").astype(bf16)
    out = out.astype(f32) + across(out).astype(f32)
    own_mixed = lax.dynamic_slice_in_dim(flat, column * share, share, 0) + out
    feat = joined_pieces(norm_rows(own_mixed).astype(bf16), "tp").reshape(rows, width)
    pred_d = jnp.dot(feat, w_dino, preferred_element_type=f32)
    pred_s = jnp.dot(feat, w_sig, preferred_element_type=f32)
    diff_d = ((pred_d - target[:, :cols_d]) * scale).astype(bf16)
    diff_s = ((pred_s - target[:, cols_d:]) * scale).astype(bf16)

    dfeat = times_transposed(diff_d, w_dino) + times_transposed(diff_s, w_sig)
    dfeat = summed_piece(dfeat.astype(bf16).reshape(count_tp, share, width), "tp")
    dmixed = joined_pieces(norm_back(own_mixed, dfeat).astype(bf16), "tp").reshape(rows, width)
    own_feat = lax.dynamic_slice_in_dim(feat, group * half, half, 1)
    grad_heads = over_rows(own_feat, jnp.concatenate([diff_d, diff_s], axis=1)).astype(bf16)
    sum_heads = summed_piece(grad_heads.reshape(count_dp, block, cols_d + cols_s), "dp")
    grad_down = over_rows(dmixed, hidden).astype(bf16)
    dhidden = jnp.dot(dmixed, w_mlp[1], preferred_element_type=f32)
    dact = (dhidden * gelu_slope(act)).astype(bf16)
    grad_up = over_rows(normed, dact).astype(bf16)

    def ordered(grad):
        return grad.reshape(2, count_dp, block, units).transpose(1, 0, 2, 3).reshape(width, units)

    grad_mlp = jnp.stack([ordered(grad_up), ordered(grad_down)])
    grad_mlp, sum_heads = lax.optimization_barrier((grad_mlp, sum_heads))
    sum_mlp = lax.psum_scatter(grad_mlp, "dp", scatter_dimension=1, tiled=True)
    sum_mlp = sum_mlp.reshape(2, 2, block, units)
    away = across(jnp.where(group == 0, sum_mlp[:, 1], sum_mlp[:, 0]).astype(bf16)).astype(f32)
    here = jnp.where(group == 0, sum_mlp[:, 0], sum_mlp[:, 1]).astype(f32)
    left = jnp.where(group == 0, here, away)
    right = jnp.where(group == 0, away, here)
    return (
        jnp.concatenate([left, right], axis=2),
        sum_heads[:, :cols_d],
        sum_heads[:, cols_d:],
    )


def solution(mesh):
    in_specs = (
        P(None, "dp", None),
        P(None, "dp", None),
        P("dp", None, None),
        P(None, "dp", "tp"),
        P(None, "dp", "tp"),
        P(None, "dp", "tp"),
        P("dp", "tp"),
        P("dp", "tp"),
        P(),
    )
    out_specs = (P(None, ("grp", "dp"), "tp"), P(("grp", "dp"), "tp"), P(("grp", "dp"), "tp"))
    return jax.shard_map(body, mesh=mesh, in_specs=in_specs, out_specs=out_specs, check_vma=False)
```

```python
import math

import jax
import jax.numpy as jnp
from jax import lax
from jax.sharding import PartitionSpec as P


def norm_rows(values):
    center = values - jnp.mean(values, axis=-1, keepdims=True)
    spread = jnp.mean(center * center, axis=-1, keepdims=True)
    return center * lax.rsqrt(spread + 1e-06)


def norm_back(values, upstream):
    center = values - jnp.mean(values, axis=-1, keepdims=True)
    factor = lax.rsqrt(jnp.mean(center * center, axis=-1, keepdims=True) + 1e-06)
    normed = center * factor
    first = jnp.mean(upstream, axis=-1, keepdims=True)
    second = jnp.mean(upstream * normed, axis=-1, keepdims=True)
    return factor * (upstream - first - normed * second)


def gelu_slope(values):
    cdf = 0.5 * (1.0 + lax.erf(values * (1.0 / math.sqrt(2.0))))
    pdf = jnp.exp(-0.5 * values * values) * (1.0 / math.sqrt(2.0 * math.pi))
    return cdf + values * pdf


def times_transposed(left, right):
    return lax.dot_general(
        left, right, (((1,), (1,)), ((), ())), preferred_element_type=jnp.float32
    )


def over_rows(left, right):
    return lax.dot_general(
        left, right, (((0,), (0,)), ((), ())), preferred_element_type=jnp.float32
    )


def gathered_rows(block, axis, held=()):
    count = lax.axis_size("dp")
    if count > 8:
        return (lax.all_gather(block, "dp", axis=axis, tiled=True), *held)
    up, down = [block], [block]
    for step in range(1, count):
        if held and step == count - 1:
            up[-1], down[-1], *held = lax.optimization_barrier((up[-1], down[-1], *held))
        up.append(lax.ppermute(up[-1], "dp", [(i, i + 1) for i in range(step - 1, count - 1)]))
        down.append(
            lax.ppermute(down[-1], "dp", [(i, i - 1) for i in range(1, count - step + 1)])
        )
    line = jnp.concatenate(up[:0:-1] + down, axis=axis)
    length = block.shape[axis]
    start = (count - 1 - lax.axis_index("dp")) * length
    return (lax.dynamic_slice_in_dim(line, start, count * length, axis), *held)


def own_units(weights, group, low):
    count = weights.shape[-1]
    return jnp.where(group == 0, weights[..., : count - low], weights[..., low:])


def summed_piece(pieces, axis):
    count = lax.axis_size(axis)
    if count > 8:
        return lax.psum_scatter(pieces, axis, scatter_dimension=0).astype(jnp.float32)
    me = lax.axis_index(axis)
    total = lax.dynamic_index_in_dim(pieces, me, 0, keepdims=False).astype(jnp.float32)
    for step in range(1, count):
        piece = lax.dynamic_index_in_dim(pieces, (me + step) % count, 0, keepdims=False)
        pairs = [(i, (i + step) % count) for i in range(count)]
        total = total + lax.ppermute(piece, axis, pairs).astype(jnp.float32)
    return total


def joined_pieces(piece, axis):
    count = lax.axis_size(axis)
    if count > 8:
        return lax.all_gather(piece, axis, axis=0)
    got = [piece]
    for step in range(1, count):
        got.append(lax.ppermute(piece, axis, [(i, (i + step) % count) for i in range(count)]))
    got = got[::-1]
    line = jnp.stack(got + got[:-1])
    return lax.dynamic_slice_in_dim(line, count - 1 - lax.axis_index(axis), count, 0)


def across(array):
    return lax.ppermute(array, "grp", [(0, 1), (1, 0)])


def body(
    dino_stream,
    siglip_stream,
    student_stream,
    dino_mlp,
    siglip_mlp,
    student_mlp,
    dino_head,
    siglip_head,
    assign,
):
    bf16, f32 = jnp.bfloat16, jnp.float32
    group = lax.axis_index("grp")
    column = lax.axis_index("tp")
    count_dp = lax.axis_size("dp")
    count_tp = lax.axis_size("tp")
    img_dev, patches, width = student_stream.shape
    rows = img_dev * patches
    images, slab, width_d = dino_stream.shape
    width_s = siglip_stream.shape[2]
    cols_d = dino_head.shape[1]
    cols_s = siglip_head.shape[1]
    units = student_mlp.shape[2] // 2
    half = width // 2
    block = half // count_dp
    scale = 1.0 / math.sqrt(images * patches)

    low_d = dino_mlp.shape[2] // 2 // 128 * 128
    low_s = siglip_mlp.shape[2] // 2 // 128 * 128
    own_dino = own_units(dino_mlp, group, low_d)
    own_siglip = own_units(siglip_mlp, group, low_s)
    own_student = own_units(student_mlp, group, units)
    w_mlp, own_dino, own_siglip = gathered_rows(own_student, 1, (own_dino, own_siglip))
    siglip_full, = gathered_rows(own_siglip, 1)
    own_heads = jnp.concatenate([dino_head, siglip_head], axis=1)
    dino_full, own_heads = gathered_rows(own_dino, 1, (own_heads,))
    w_heads, = gathered_rows(own_heads, 0)

    def once(hidden, low):
        place = lax.broadcasted_iota(jnp.int32, hidden.shape, 1)
        return jnp.where((group == 1) | (place < low), hidden, jnp.zeros_like(hidden))

    normed_d = norm_rows(dino_stream.reshape(images * slab, width_d).astype(f32)).astype(bf16)
    gate = jnp.dot(normed_d, dino_full[0], preferred_element_type=f32)
    upper = jnp.dot(normed_d, dino_full[1], preferred_element_type=f32)
    hidden_d = once((jax.nn.silu(gate) * upper).astype(bf16), low_d)
    part_d = times_transposed(hidden_d, dino_full[2]).astype(bf16)
    normed_s = norm_rows(siglip_stream.reshape(images * slab, width_s).astype(f32)).astype(bf16)
    first = jnp.dot(normed_s, siglip_full[0], preferred_element_type=f32)
    hidden_s = once(jax.nn.gelu(first, approximate=True).astype(bf16), low_s)
    part_s = times_transposed(hidden_s, siglip_full[1]).astype(bf16)
    parts = jnp.stack(
        [
            jnp.concatenate(
                [
                    part_d[:, i * cols_d : (i + 1) * cols_d],
                    part_s[:, i * cols_s : (i + 1) * cols_s],
                ],
                axis=1,
            )
            for i in range(count_tp)
        ]
    )
    summed = summed_piece(parts, "tp").astype(bf16)
    summed = summed.astype(f32) + across(summed).astype(f32)
    own = jnp.concatenate(
        [
            lax.dynamic_slice_in_dim(dino_stream, column * cols_d, cols_d, 2),
            lax.dynamic_slice_in_dim(siglip_stream, column * cols_s, cols_s, 2),
        ],
        axis=2,
    )
    features = (own.astype(f32) + summed.reshape(own.shape)).astype(bf16)
    arranged = jnp.take(features, assign, axis=0)
    target = lax.all_to_all(arranged, "dp", split_axis=0, concat_axis=1, tiled=True)
    target = target.reshape(rows, cols_d + cols_s).astype(f32)

    flat = student_stream.reshape(rows, width).astype(f32)
    normed = norm_rows(flat).astype(bf16)
    act = jnp.dot(normed, w_mlp[0], preferred_element_type=f32)
    hidden = jax.nn.gelu(act, approximate=False).astype(bf16)
    partial_out = times_transposed(hidden, w_mlp[1])
    share = rows // count_tp
    out = summed_piece(partial_out.astype(bf16).reshape(count_tp, share, width), "tp").astype(bf16)
    out = out.astype(f32) + across(out).astype(f32)
    own_mixed = lax.dynamic_slice_in_dim(flat, column * share, share, 0) + out
    feat = joined_pieces(norm_rows(own_mixed).astype(bf16), "tp").reshape(rows, width)
    pred = jnp.dot(feat, w_heads, preferred_element_type=f32)
    diff = ((pred - target) * scale).astype(bf16)

    dfeat = times_transposed(diff, w_heads)
    dfeat = summed_piece(dfeat.astype(bf16).reshape(count_tp, share, width), "tp")
    dmixed = joined_pieces(norm_back(own_mixed, dfeat).astype(bf16), "tp").reshape(rows, width)
    own_feat = lax.dynamic_slice_in_dim(feat, group * half, half, 1)
    grad_heads = over_rows(own_feat, diff).astype(bf16)
    sum_heads = summed_piece(grad_heads.reshape(count_dp, block, cols_d + cols_s), "dp")
    grad_down = over_rows(dmixed, hidden).astype(bf16)
    dhidden = jnp.dot(dmixed, w_mlp[1], preferred_element_type=f32)
    dact = (dhidden * gelu_slope(act)).astype(bf16)
    grad_up = over_rows(normed, dact).astype(bf16)

    def ordered(grad):
        return grad.reshape(2, count_dp, block, units).transpose(1, 0, 2, 3).reshape(width, units)

    grad_mlp = jnp.stack([ordered(grad_up), ordered(grad_down)])
    grad_mlp, sum_heads = lax.optimization_barrier((grad_mlp, sum_heads))
    sum_mlp = lax.psum_scatter(grad_mlp, "dp", scatter_dimension=1, tiled=True)
    sum_mlp = sum_mlp.reshape(2, 2, block, units)
    away = across(jnp.where(group == 0, sum_mlp[:, 1], sum_mlp[:, 0]).astype(bf16)).astype(f32)
    here = jnp.where(group == 0, sum_mlp[:, 0], sum_mlp[:, 1]).astype(f32)
    left = jnp.where(group == 0, here, away)
    right = jnp.where(group == 0, away, here)
    return (
        jnp.concatenate([left, right], axis=2),
        sum_heads[:, :cols_d],
        sum_heads[:, cols_d:],
    )


def solution(mesh):
    in_specs = (
        P(None, "dp", None),
        P(None, "dp", None),
        P("dp", None, None),
        P(None, "dp", "tp"),
        P(None, "dp", "tp"),
        P(None, "dp", "tp"),
        P("dp", "tp"),
        P("dp", "tp"),
        P(),
    )
    out_specs = (P(None, ("grp", "dp"), "tp"), P(("grp", "dp"), "tp"), P(("grp", "dp"), "tp"))
    return jax.shard_map(body, mesh=mesh, in_specs=in_specs, out_specs=out_specs, check_vma=False)
```
